512 devices in a mesh: wide: 64 (over z_lo, x, y), narrow: 8 (over z_hi, core).
Axes of the slice: x: 4, y: 8, z: 8 (z_hi: 4, z_lo: 2; z = z_hi * 2 + z_lo), core: 2. Of those that a mesh axis runs over, the one named last changes fastest.
Arguments:
- points: bfloat16 [65536, 256], P(('wide', 'narrow')), may hold values from -8 to 8
- log_point_weight: float32 [65536], P(('wide', 'narrow')), may hold values from -4 to 4
- potential: float32 [65536], P(('wide', 'narrow')), may hold values from -12 to 503
Outputs:
- new_potential: float32 [65536], P(('wide', 'narrow'))
- residual_norm: float32 [], replicated
The draws below stay inside these ranges and needn't reach their ends.
All inputs are finite; a program needn't handle non-finite values.
Results may differ from the reference program's by a relative error of at most 0.0003.
Values may be sent and summed in bfloat16 or wider, within the bound.
No kernel may reach another device: no remote copies, remote signals or barrier semaphores. Data moves between devices by JAX's collectives and lax.ppermute only.
A program may use at most 64 MiB of HBM per device.

```python
import math
import jax
import jax.numpy as jnp
from jax import lax

F = 256
NPTS = 65536


def draw_points(key, part):
    key = jax.random.fold_in(key, 1)
    member = jax.random.randint(jax.random.fold_in(key, 7), (NPTS,), 0, 64)
    centres = 0.25 * jax.random.truncated_normal(jax.random.fold_in(key, 3), -4.0, 4.0, (64, F), jnp.float32)
    noise = 0.15 * jax.random.truncated_normal(key, -4.0, 4.0, (NPTS, F), jnp.float32)
    values = centres[member] + noise
    return values.astype(jnp.bfloat16)


def draw_potential(key, part):
    key = jax.random.fold_in(key, 2)
    position = jnp.arange(NPTS, dtype=jnp.float32) / NPTS
    spread = 0.3 * jnp.power(10.0, position)
    values = jax.random.truncated_normal(key, -4.0, 4.0, (NPTS,), jnp.float32) * spread
    return values


def steps_of(own_key, shape, shards, least, largest):
    def one(dim, blocks):
        draws = jax.random.uniform(jax.random.fold_in(jax.random.fold_in(own_key, 6), dim), (blocks,), jnp.float32, least / len(shards), largest / len(shards))
        return jnp.repeat(jnp.exp(draws), shape[dim] // blocks).reshape((-1,) + (1,) * (len(shape) - dim - 1))

    level = one(*shards[0])
    for cut in shards[1:]:
        level = level * one(*cut)
    return level


def normal_values(key, dims, deviation, bound, cuts=(), held_as=jnp.bfloat16):
    level = steps_of(key, dims, cuts, -0.22, 0.18) if cuts else 1.0
    result = jax.random.normal(key, dims, jnp.float32) * deviation * level
    return jnp.minimum(jnp.maximum(result, -bound), bound).astype(held_as)


def setup_inputs(seed: int = 0) -> dict:
    key_list = jax.random.split(jax.random.key(seed), 4)
    return {
        "points": draw_points(jax.random.fold_in(key_list[3], 71), 0),
        "log_point_weight": normal_values(key_list[1], (NPTS,), 1.0, 4.0, ((0, 512),), jnp.float32),
        "potential": draw_potential(jax.random.fold_in(key_list[3], 71), 0),
    }


entropic_epsilon = 2.0

def reference(points, log_point_weight, potential):
    squared_norms = lax.optimization_barrier(jnp.sum(jnp.square(points.astype(jnp.float32)), axis=1))
    offset_scores = log_point_weight + potential / entropic_epsilon - 0.5 * squared_norms / entropic_epsilon
    block_rows = math.gcd(NPTS, 512)
    grouped = points.reshape(NPTS // block_rows, block_rows, F)

    def row_block(block_points):
        inner_products = jnp.dot(block_points, points.T, preferred_element_type=jnp.float32)
        kernel_scores = offset_scores[None, :] + inner_products / entropic_epsilon
        highest = lax.optimization_barrier(jnp.max(kernel_scores, axis=1))
        return highest + jnp.log(lax.optimization_barrier(jnp.sum(jnp.exp(kernel_scores - highest[:, None]), axis=1)))
    log_normalizer = lax.map(row_block, grouped).reshape(NPTS)
    refreshed_potential = 0.5 * squared_norms - entropic_epsilon * log_normalizer
    new_potential = 0.5 * (potential + refreshed_potential)
    change = refreshed_potential - potential
    residual_norm = jnp.sqrt(jnp.sum(change * change) / NPTS + 1e-06)
    return (new_potential, residual_norm)
```

```python
import math

import jax
import jax.numpy as jnp
from jax import lax
from jax.experimental import pallas as pl
from jax.experimental.pallas import tpu as pltpu
from jax.sharding import PartitionSpec as P

LOG2E = math.log2(math.e)
LN2 = math.log(2.0)
AXES = ("wide", "narrow")
SHAPE = (2, 2, 2, 8, 4, 2)
MEMBERS = 16
LOCAL = 128
TAIL = 16
MESSAGE = 2 * LOCAL + TAIL
VMEM = 56 * 1024 * 1024


def index(z_lo, x_hi, x_lo, y, z_hi, core):
    where = 0
    for size, at in zip(SHAPE, (z_lo, x_hi, x_lo, y, z_hi, core)):
        where = where * size + at
    return where


def row_groups(cores):
    return [
        [index(a, b, c, y, h, core) for c in range(2) for y in range(8)]
        for a in range(2)
        for b in range(2)
        for h in range(4)
        for core in cores
    ]


def column_groups(cores):
    return [
        [index(a, b, c, y, h, core) for b in range(2) for h in range(4) for a in range(2)]
        for c in range(2)
        for y in range(8)
        for core in cores
    ]


def remaining_groups():
    return [
        [
            index(a, b, c, y, h, core)
            for b in range(2)
            for h in range(4)
            for a in range(2)
            for core in range(2)
        ]
        for c in range(2)
        for y in range(8)
    ]


def three_terms(value):
    high = value.astype(jnp.bfloat16).astype(jnp.float32)
    rest = value - high
    middle = rest.astype(jnp.bfloat16).astype(jnp.float32)
    return high, middle, rest - middle


def pack_kernel(points_ref, weight_ref, potential_ref, out_ref):
    points = points_ref[...]
    wide = points.astype(jnp.float32)
    square = wide * wide
    high = square.astype(jnp.bfloat16)
    low = (square - high.astype(jnp.float32)).astype(jnp.bfloat16)
    ones = jnp.ones((8, points.shape[1]), jnp.bfloat16)
    dims = (((1,), (1,)), ((), ()))
    norms = lax.dot_general(ones, high, dims, preferred_element_type=jnp.float32)
    norms = norms + lax.dot_general(ones, low, dims, preferred_element_type=jnp.float32)
    norms = norms[:1]
    potential = potential_ref[...]
    offset = weight_ref[...] + 0.5 * potential - 0.25 * norms
    rows = [
        jnp.concatenate([a, b], axis=1)
        for a, b in zip(three_terms(offset * LOG2E), three_terms(0.5 * norms - potential))
    ]
    half = jnp.concatenate(rows + [jnp.zeros((5, 2 * LOCAL), jnp.float32)], axis=0)
    out_ref[:LOCAL] = points
    out_ref[LOCAL:] = jnp.concatenate([half, half], axis=0).astype(jnp.bfloat16)


def spread_kernel(pair_ref, out_ref):
    stride = LOCAL + TAIL
    first, second = pair_ref[LOCAL:stride], pair_ref[stride + LOCAL :]
    row = lax.broadcasted_iota(jnp.int32, first.shape, 0)
    tail = jnp.where(row < 8, first.astype(jnp.float32), second.astype(jnp.float32))
    tail = tail.astype(jnp.bfloat16)
    for member in range(MEMBERS):
        out_ref[member, :LOCAL] = pair_ref[:LOCAL]
        out_ref[member, LOCAL : 2 * LOCAL] = pair_ref[stride : stride + LOCAL]
        out_ref[member, 2 * LOCAL :] = tail


def pairs_kernel(
    core_ref, own_ref, other_ref, sum_ref, base_ref, rows, row_tail, columns, offsets, sems
):
    core = core_ref[0]

    def copies(row_source, column_source):
        return (
            pltpu.make_async_copy(
                row_source.at[:, pl.ds(pl.multiple_of(core * LOCAL, LOCAL), LOCAL)], rows, sems.at[0]
            ),
            pltpu.make_async_copy(row_source.at[:, pl.ds(2 * LOCAL, TAIL)], row_tail, sems.at[1]),
            pltpu.make_async_copy(column_source, columns, sems.at[2]),
        )

    @pl.when(core == 0)
    def _():
        for copy in copies(own_ref, other_ref):
            copy.start()

    @pl.when(core == 1)
    def _():
        for copy in copies(other_ref, own_ref):
            copy.start()

    for copy in copies(own_ref, other_ref):
        copy.wait()

    tails = row_tail[...].astype(jnp.float32)[:, :, LOCAL:]
    half = lax.broadcasted_iota(jnp.int32, tails.shape, 1) // 8
    base_ref[...] = jnp.sum(jnp.where(half == core, tails, 0.0), axis=1)

    half = lax.broadcasted_iota(jnp.int32, (TAIL, LOCAL), 0) // 8
    for member in range(MEMBERS):
        tail = columns[member, 2 * LOCAL :, :LOCAL]
        for side in range(2):
            pick = jnp.where(half == side, 1.0, 0.0).astype(jnp.bfloat16)
            offsets[member, side * LOCAL : (side + 1) * LOCAL] = lax.dot_general(
                tail, pick, (((0,), (0,)), ((), ())), preferred_element_type=jnp.float32
            )

    scale = 0.5 * LOG2E

    def row_step(step, unused):
        mine = rows[pl.ds(2 * step, 2)].reshape(2 * LOCAL, -1)
        highest = total = None
        for member in range(MEMBERS):
            inner = lax.dot_general(
                columns[member, : 2 * LOCAL],
                mine,
                (((1,), (1,)), ((), ())),
                preferred_element_type=jnp.float32,
            )
            shift = offsets[member]
            score = inner * scale + jnp.concatenate([shift, shift], axis=1)
            score = score.reshape(2 * LOCAL // 8, 8, 2 * LOCAL)
            top = jnp.max(score, axis=0)
            if member:
                top = jnp.maximum(top, highest)
            part = jnp.sum(jnp.exp2(score - top[None]), axis=0)
            total = part if member == 0 else part + total * jnp.exp2(highest - top)
            highest = top
        top = jnp.max(highest, axis=0, keepdims=True)
        total = jnp.sum(total * jnp.exp2(highest - top), axis=0, keepdims=True)
        value = top + jnp.log2(total)
        sum_ref[pl.ds(2 * step, 1)] = value[:, :LOCAL]
        sum_ref[pl.ds(2 * step + 1, 1)] = value[:, LOCAL:]
        return unused

    lax.fori_loop(0, MEMBERS // 2, row_step, 0)


def finish_kernel(place_ref, parts_ref, base_ref, potential_ref, new_ref, change_ref):
    parts = parts_ref[...]
    top = jnp.max(parts, axis=0)
    value = top + jnp.log2(jnp.sum(jnp.exp2(parts - top[None]), axis=0))
    change = base_ref[...] - (2.0 * LN2) * value
    row = lax.broadcasted_iota(jnp.int32, change.shape, 0)
    mine = jnp.sum(jnp.where(row == place_ref[0], change, 0.0), axis=0, keepdims=True)
    new_ref[...] = potential_ref[...] + 0.5 * mine
    whole = jnp.sum(jnp.sum(change * change, axis=0, keepdims=True), axis=1, keepdims=True)
    change_ref[...] = jnp.broadcast_to(whole, change_ref.shape)


def norm_kernel(count, parts_ref, out_ref):
    whole = jnp.sum(parts_ref[...], axis=0, keepdims=True)
    out_ref[...] = jnp.sqrt(whole / count + 1e-06)


def call(kernel, outs, *operands, **options):
    return pl.pallas_call(
        kernel,
        out_shape=outs,
        compiler_params=pltpu.CompilerParams(vmem_limit_bytes=VMEM),
        **options,
    )(*operands)


IN_VMEM = pl.BlockSpec(memory_space=pltpu.VMEM)
IN_SMEM = pl.BlockSpec(memory_space=pltpu.SMEM)
ANYWHERE = pl.BlockSpec(memory_space=pl.ANY)


def shape(*dims, dtype=jnp.float32):
    return jax.ShapeDtypeStruct(dims, dtype)


def per_device(points, log_point_weight, potential):
    features = points.shape[1]
    narrow = lax.axis_size("narrow")
    core = lax.axis_index("narrow") % 2
    place = lax.axis_index("wide") % MEMBERS
    own_potential = potential.reshape(1, LOCAL)
    packed = call(
        pack_kernel,
        shape(LOCAL + TAIL, features, dtype=jnp.bfloat16),
        points,
        log_point_weight.reshape(1, LOCAL),
        own_potential,
    )
    pair = lax.all_gather(
        packed,
        "narrow",
        axis=0,
        tiled=True,
        axis_index_groups=[[at, at + 1] for at in range(0, narrow, 2)],
    )
    message = call(
        spread_kernel, shape(MEMBERS, MESSAGE, features, dtype=jnp.bfloat16), pair
    )
    own = lax.all_to_all(
        message,
        AXES,
        0,
        0,
        tiled=True,
        axis_index_groups=row_groups([0]) + column_groups([1]),
    )
    other = lax.ppermute(own, "narrow", [(at, at ^ 1) for at in range(narrow)])
    sums, base = call(
        pairs_kernel,
        (shape(MEMBERS, LOCAL), shape(MEMBERS, LOCAL)),
        core.reshape(1),
        own,
        other,
        in_specs=[IN_SMEM, ANYWHERE, ANYWHERE],
        out_specs=[IN_VMEM, IN_VMEM],
        scratch_shapes=[
            pltpu.VMEM((MEMBERS, LOCAL, features), jnp.bfloat16),
            pltpu.VMEM((MEMBERS, TAIL, features), jnp.bfloat16),
            pltpu.VMEM((MEMBERS, MESSAGE, features), jnp.bfloat16),
            pltpu.VMEM((MEMBERS, 2 * LOCAL, LOCAL), jnp.float32),
            pltpu.SemaphoreType.DMA((3,)),
        ],
    )
    parts = lax.all_to_all(
        jnp.broadcast_to(sums[None], (MEMBERS, MEMBERS, LOCAL)),
        AXES,
        0,
        0,
        tiled=True,
        axis_index_groups=row_groups([0, 1]),
    )
    new_potential, change = call(
        finish_kernel,
        (shape(1, LOCAL), shape(2 * MEMBERS, LOCAL)),
        place.reshape(1),
        parts,
        base,
        own_potential,
        in_specs=[IN_SMEM, IN_VMEM, IN_VMEM, IN_VMEM],
        out_specs=[IN_VMEM, IN_VMEM],
    )
    changes = lax.all_to_all(
        change, AXES, 0, 0, tiled=True, axis_index_groups=remaining_groups()
    )
    count = LOCAL * lax.axis_size(AXES)
    norm = call(lambda a, b: norm_kernel(count, a, b), shape(1, LOCAL), changes)
    return new_potential.reshape(LOCAL), norm[0, 0]


def solution(mesh):
    in_specs = (P(AXES, None), P(AXES), P(AXES))
    out_specs = (P(AXES), P())
    return jax.shard_map(
        per_device, mesh=mesh, in_specs=in_specs, out_specs=out_specs, check_vma=False
    )
```

```python
import math

import jax
import jax.numpy as jnp
from jax import lax
from jax.experimental import pallas as pl
from jax.experimental.pallas import tpu as pltpu
from jax.sharding import PartitionSpec as P

LOG2E = math.log2(math.e)
LN2 = math.log(2.0)
AXES = ("wide", "narrow")
SHAPE = (2, 4, 8, 4, 2)
MEMBERS = 16
LOCAL = 128
TAIL = 16
MESSAGE = 2 * LOCAL + TAIL
MIB = 1024 * 1024
PAIRS = ((0, 1), (2, 3))
CROSS = ((1, 2), (3, 0))


def index(x, y, z, core):
    where = 0
    for size, at in zip(SHAPE, (z % 2, x, y, z // 2, core)):
        where = where * size + at
    return where


def row_groups(cores):
    return [
        [index(x, y, z, core) for x in pair for y in range(8)]
        for pair in PAIRS
        for z in range(8)
        for core in cores
    ]


def column_groups(cores):
    return [
        [index(x, y, z, core) for x in pair for z in range(8)]
        for pair in CROSS
        for y in range(8)
        for core in cores
    ]


def remaining_groups():
    return [
        [index(x, y, z, core) for x in pair for z in range(8) for core in range(2)]
        for pair in CROSS
        for y in range(8)
    ]


def three_terms(value):
    high = value.astype(jnp.bfloat16).astype(jnp.float32)
    rest = value - high
    middle = rest.astype(jnp.bfloat16).astype(jnp.float32)
    return high, middle, rest - middle


def pack_kernel(points_ref, weight_ref, potential_ref, out_ref):
    points = points_ref[...]
    wide = points.astype(jnp.float32)
    square = wide * wide
    high = square.astype(jnp.bfloat16)
    low = (square - high.astype(jnp.float32)).astype(jnp.bfloat16)
    ones = jnp.ones((8, points.shape[1]), jnp.bfloat16)
    dims = (((1,), (1,)), ((), ()))
    norms = lax.dot_general(ones, high, dims, preferred_element_type=jnp.float32)
    norms = norms + lax.dot_general(ones, low, dims, preferred_element_type=jnp.float32)
    norms = norms[:1]
    potential = potential_ref[...]
    offset = weight_ref[...] + 0.5 * potential - 0.25 * norms
    rows = [
        jnp.concatenate([a, b], axis=1)
        for a, b in zip(three_terms(offset * LOG2E), three_terms(0.5 * norms - potential))
    ]
    half = jnp.concatenate(rows + [jnp.zeros((5, 2 * LOCAL), jnp.float32)], axis=0)
    out_ref[:LOCAL] = points
    out_ref[LOCAL:] = jnp.concatenate([half, half], axis=0).astype(jnp.bfloat16)


def spread_kernel(pair_ref, out_ref):
    stride = LOCAL + TAIL
    first, second = pair_ref[LOCAL:stride], pair_ref[stride + LOCAL :]
    row = lax.broadcasted_iota(jnp.int32, first.shape, 0)
    tail = jnp.where(row < 8, first.astype(jnp.float32), second.astype(jnp.float32))
    tail = tail.astype(jnp.bfloat16)
    for member in range(MEMBERS):
        out_ref[member, :LOCAL] = pair_ref[:LOCAL]
        out_ref[member, LOCAL : 2 * LOCAL] = pair_ref[stride : stride + LOCAL]
        out_ref[member, 2 * LOCAL :] = tail


def pairs_kernel(
    core_ref, own_ref, other_ref, sum_ref, base_ref, rows, row_tail, columns, offsets, sems
):
    core = core_ref[0]

    def copies(row_source, column_source):
        return (
            pltpu.make_async_copy(
                row_source.at[:, pl.ds(pl.multiple_of(core * LOCAL, LOCAL), LOCAL)], rows, sems.at[0]
            ),
            pltpu.make_async_copy(row_source.at[:, pl.ds(2 * LOCAL, TAIL)], row_tail, sems.at[1]),
            pltpu.make_async_copy(column_source, columns, sems.at[2]),
        )

    @pl.when(core == 0)
    def _():
        for copy in copies(own_ref, other_ref):
            copy.start()

    @pl.when(core == 1)
    def _():
        for copy in copies(other_ref, own_ref):
            copy.start()

    for copy in copies(own_ref, other_ref):
        copy.wait()

    tails = row_tail[...].astype(jnp.float32)[:, :, LOCAL:]
    half = lax.broadcasted_iota(jnp.int32, tails.shape, 1) // 8
    base_ref[...] = jnp.sum(jnp.where(half == core, tails, 0.0), axis=1)

    half = lax.broadcasted_iota(jnp.int32, (TAIL, LOCAL), 0) // 8
    for member in range(MEMBERS):
        tail = columns[member, 2 * LOCAL :, :LOCAL]
        for side in range(2):
            pick = jnp.where(half == side, 1.0, 0.0).astype(jnp.bfloat16)
            offsets[member, side * LOCAL : (side + 1) * LOCAL] = lax.dot_general(
                tail, pick, (((0,), (0,)), ((), ())), preferred_element_type=jnp.float32
            )

    scale = 0.5 * LOG2E

    def row_step(step, unused):
        mine = rows[pl.ds(2 * step, 2)].reshape(2 * LOCAL, -1)
        highest = total = None
        for member in range(MEMBERS):
            inner = lax.dot_general(
                columns[member, : 2 * LOCAL],
                mine,
                (((1,), (1,)), ((), ())),
                preferred_element_type=jnp.float32,
            )
            shift = offsets[member]
            score = inner * scale + jnp.concatenate([shift, shift], axis=1)
            score = score.reshape(2 * LOCAL // 8, 8, 2 * LOCAL)
            top = jnp.max(score, axis=0)
            if member:
                top = jnp.maximum(top, highest)
            part = jnp.sum(jnp.exp2(score - top[None]), axis=0)
            total = part if member == 0 else part + total * jnp.exp2(highest - top)
            highest = top
        top = jnp.max(highest, axis=0, keepdims=True)
        total = jnp.sum(total * jnp.exp2(highest - top), axis=0, keepdims=True)
        value = top + jnp.log2(total)
        for member in range(MEMBERS):
            sum_ref[member, pl.ds(2 * step, 1)] = value[:, :LOCAL]
            sum_ref[member, pl.ds(2 * step + 1, 1)] = value[:, LOCAL:]
        return unused

    lax.fori_loop(0, MEMBERS // 2, row_step, 0)


def finish_kernel(place_ref, parts_ref, base_ref, potential_ref, new_ref, change_ref):
    parts = parts_ref[...]
    top = jnp.max(parts, axis=0)
    value = top + jnp.log2(jnp.sum(jnp.exp2(parts - top[None]), axis=0))
    change = base_ref[...] - (2.0 * LN2) * value
    row = lax.broadcasted_iota(jnp.int32, change.shape, 0)
    mine = jnp.sum(jnp.where(row == place_ref[0], change, 0.0), axis=0, keepdims=True)
    new_ref[...] = potential_ref[...] + 0.5 * mine
    whole = jnp.sum(jnp.sum(change * change, axis=0, keepdims=True), axis=1, keepdims=True)
    change_ref[...] = jnp.broadcast_to(whole, change_ref.shape)


def norm_kernel(count, parts_ref, out_ref):
    whole = jnp.sum(parts_ref[...], axis=0, keepdims=True)
    out_ref[...] = jnp.sqrt(whole / count + 1e-06)


def call(kernel, outs, *operands, limit=4, **options):
    return pl.pallas_call(
        kernel,
        out_shape=outs,
        compiler_params=pltpu.CompilerParams(vmem_limit_bytes=limit * MIB),
        **options,
    )(*operands)


IN_VMEM = pl.BlockSpec(memory_space=pltpu.VMEM)
IN_SMEM = pl.BlockSpec(memory_space=pltpu.SMEM)
ANYWHERE = pl.BlockSpec(memory_space=pl.ANY)


def shape(*dims, dtype=jnp.float32):
    return jax.ShapeDtypeStruct(dims, dtype)


def per_device(points, log_point_weight, potential):
    features = points.shape[1]
    narrow = lax.axis_size("narrow")
    core = lax.axis_index("narrow") % 2
    place = lax.axis_index("wide") % MEMBERS
    own_potential = potential.reshape(1, LOCAL)
    packed = call(
        pack_kernel,
        shape(LOCAL + TAIL, features, dtype=jnp.bfloat16),
        points,
        log_point_weight.reshape(1, LOCAL),
        own_potential,
    )
    pair = lax.all_gather(
        packed,
        "narrow",
        axis=0,
        tiled=True,
        axis_index_groups=[[at, at + 1] for at in range(0, narrow, 2)],
    )
    message = call(
        spread_kernel, shape(MEMBERS, MESSAGE, features, dtype=jnp.bfloat16), pair, limit=8
    )
    own = lax.all_to_all(
        message,
        AXES,
        0,
        0,
        tiled=True,
        axis_index_groups=row_groups([0]) + column_groups([1]),
    )
    other = lax.ppermute(own, "narrow", [(at, at ^ 1) for at in range(narrow)])
    sums, base = call(
        pairs_kernel,
        (shape(MEMBERS, MEMBERS, LOCAL), shape(MEMBERS, LOCAL)),
        core.reshape(1),
        own,
        other,
        limit=24,
        in_specs=[IN_SMEM, ANYWHERE, ANYWHERE],
        out_specs=[IN_VMEM, IN_VMEM],
        scratch_shapes=[
            pltpu.VMEM((MEMBERS, LOCAL, features), jnp.bfloat16),
            pltpu.VMEM((MEMBERS, TAIL, features), jnp.bfloat16),
            pltpu.VMEM((MEMBERS, MESSAGE, features), jnp.bfloat16),
            pltpu.VMEM((MEMBERS, 2 * LOCAL, LOCAL), jnp.float32),
            pltpu.SemaphoreType.DMA((3,)),
        ],
    )
    parts = lax.all_to_all(
        sums,
        AXES,
        0,
        0,
        tiled=True,
        axis_index_groups=row_groups([0, 1]),
    )
    new_potential, change = call(
        finish_kernel,
        (shape(1, LOCAL), shape(2 * MEMBERS, LOCAL)),
        place.reshape(1),
        parts,
        base,
        own_potential,
        in_specs=[IN_SMEM, IN_VMEM, IN_VMEM, IN_VMEM],
        out_specs=[IN_VMEM, IN_VMEM],
    )
    changes = lax.all_to_all(
        change, AXES, 0, 0, tiled=True, axis_index_groups=remaining_groups()
    )
    count = LOCAL * lax.axis_size(AXES)
    norm = call(lambda a, b: norm_kernel(count, a, b), shape(1, LOCAL), changes)
    return new_potential.reshape(LOCAL), norm[0, 0]


def solution(mesh):
    in_specs = (P(AXES, None), P(AXES), P(AXES))
    out_specs = (P(AXES), P())
    return jax.shard_map(
        per_device, mesh=mesh, in_specs=in_specs, out_specs=out_specs, check_vma=False
    )
```

```python
import math

import jax
import jax.numpy as jnp
from jax import lax
from jax.experimental import pallas as pl
from jax.experimental.pallas import tpu as pltpu
from jax.sharding import PartitionSpec as P

LOG2E = math.log2(math.e)
LN2 = math.log(2.0)
AXES = ("wide", "narrow")
SHAPE = (2, 4, 8, 4, 2)
MEMBERS = 16
LOCAL = 128
TAIL = 16
TILE = 4
MESSAGE = 2 * LOCAL + TAIL
MIB = 1024 * 1024
PAIRS = ((0, 1), (2, 3))
CROSS = ((1, 2), (3, 0))


def index(x, y, z, core):
    where = 0
    for size, at in zip(SHAPE, (z % 2, x, y, z // 2, core)):
        where = where * size + at
    return where


def row_groups(cores):
    return [
        [index(x, y, z, core) for x in pair for y in range(8)]
        for pair in PAIRS
        for z in range(8)
        for core in cores
    ]


def column_groups(cores):
    return [
        [index(x, y, z, core) for x in pair for z in range(8)]
        for pair in CROSS
        for y in range(8)
        for core in cores
    ]


def remaining_groups():
    return [
        [index(x, y, z, core) for x in pair for z in range(8) for core in range(2)]
        for pair in CROSS
        for y in range(8)
    ]


def three_terms(value):
    high = value.astype(jnp.bfloat16).astype(jnp.float32)
    rest = value - high
    middle = rest.astype(jnp.bfloat16).astype(jnp.float32)
    return high, middle, rest - middle


def pack_kernel(points_ref, weight_ref, potential_ref, out_ref):
    points = points_ref[...]
    wide = points.astype(jnp.float32)
    square = wide * wide
    high = square.astype(jnp.bfloat16)
    low = (square - high.astype(jnp.float32)).astype(jnp.bfloat16)
    ones = jnp.ones((8, points.shape[1]), jnp.bfloat16)
    dims = (((1,), (1,)), ((), ()))
    norms = lax.dot_general(ones, high, dims, preferred_element_type=jnp.float32)
    norms = norms + lax.dot_general(ones, low, dims, preferred_element_type=jnp.float32)
    norms = norms[:1]
    potential = potential_ref[...]
    mass = weight_ref[...] + 0.5 * potential
    offset = (mass - 0.25 * norms) * LOG2E
    own_term = (mass + 0.25 * norms) * LOG2E
    left = three_terms(offset) + three_terms(mass * LOG2E)
    right = three_terms(0.5 * norms - potential) + three_terms(own_term)
    rows = [jnp.concatenate(both, axis=1) for both in zip(left, right)]
    half = jnp.concatenate(rows + [jnp.zeros((2, 2 * LOCAL), jnp.float32)], axis=0)
    out_ref[:LOCAL] = points
    out_ref[LOCAL:] = jnp.concatenate([half, half], axis=0).astype(jnp.bfloat16)


def spread_kernel(pair_ref, out_ref):
    stride = LOCAL + TAIL
    first, second = pair_ref[LOCAL:stride], pair_ref[stride + LOCAL :]
    row = lax.broadcasted_iota(jnp.int32, first.shape, 0)
    tail = jnp.where(row < 8, first.astype(jnp.float32), second.astype(jnp.float32))
    tail = tail.astype(jnp.bfloat16)
    for member in range(MEMBERS):
        out_ref[member, :LOCAL] = pair_ref[:LOCAL]
        out_ref[member, LOCAL : 2 * LOCAL] = pair_ref[stride : stride + LOCAL]
        out_ref[member, 2 * LOCAL :] = tail


def pairs_kernel(
    core_ref, own_ref, other_ref, sum_ref, base_ref, rows, row_tail, columns, offsets, sems
):
    core = core_ref[0]

    def copies(row_source, column_source):
        mine = pl.ds(pl.multiple_of(core * LOCAL, LOCAL), LOCAL)
        points, tail = pl.ds(0, 2 * LOCAL), pl.ds(2 * LOCAL, TAIL)
        plan = [
            (row_source.at[:, tail], row_tail),
            (column_source.at[:, tail], columns.at[:, tail]),
            (row_source.at[:, mine], rows),
            (column_source.at[:, points], columns.at[:, points]),
        ]
        return [
            pltpu.make_async_copy(source, target, sems.at[at])
            for at, (source, target) in enumerate(plan)
        ]

    @pl.when(core == 0)
    def _():
        for copy in copies(own_ref, other_ref):
            copy.start()

    @pl.when(core == 1)
    def _():
        for copy in copies(other_ref, own_ref):
            copy.start()

    waits = copies(own_ref, other_ref)
    waits[0].wait()
    waits[1].wait()

    half = lax.broadcasted_iota(jnp.int32, (MEMBERS, 8, LOCAL), 1)

    def gather(tail, first):
        pick = (half >= first) & (half < first + 3)
        return jnp.sum(jnp.where(pick, tail, 0.0), axis=1)

    tails = row_tail[...].astype(jnp.float32)
    tails = jnp.where(core == 0, tails[:, :8], tails[:, 8:])
    base_ref[...] = gather(tails[:, :, LOCAL:], 0)
    own_term = gather(tails[:, :, LOCAL:], 3)
    least = jnp.min(own_term)
    quarter = jnp.max(own_term - gather(tails[:, :, :LOCAL], 3))
    tails = columns[:, 2 * LOCAL :, :LOCAL].astype(jnp.float32)
    mass = jnp.max(jnp.maximum(gather(tails[:, :8], 3), gather(tails[:, 8:], 3)))
    near = mass + quarter - least <= 200.0
    shift = jnp.where(near, least + 90.0, 0.0)

    row = lax.broadcasted_iota(jnp.int32, (TAIL, LOCAL), 0)
    for member in range(MEMBERS):
        tail = columns[member, 2 * LOCAL :, :LOCAL]
        for side in range(2):
            pick = (row >= 8 * side) & (row < 8 * side + 3)
            offsets[member, side * LOCAL : (side + 1) * LOCAL] = lax.dot_general(
                tail,
                jnp.where(pick, 1.0, 0.0).astype(jnp.bfloat16),
                (((0,), (0,)), ((), ())),
                preferred_element_type=jnp.float32,
            ) - shift

    waits[2].wait()
    waits[3].wait()

    def scores(member, mine):
        inner = lax.dot_general(
            columns[member, : 2 * LOCAL],
            mine,
            (((1,), (1,)), ((), ())),
            preferred_element_type=jnp.float32,
        )
        score = inner * (0.5 * LOG2E) + jnp.concatenate([offsets[member]] * TILE, axis=1)
        return score.reshape(2 * LOCAL // 8, 8, TILE * LOCAL)

    def store(step, value):
        for block in range(TILE):
            line = value[:, block * LOCAL : (block + 1) * LOCAL]
            for member in range(MEMBERS):
                sum_ref[member, pl.ds(step * TILE + block, 1)] = line

    def tile(step):
        return rows[pl.ds(step * TILE, TILE)].reshape(TILE * LOCAL, -1)

    def one_shift(step):
        mine = tile(step)
        total = jnp.zeros((8, TILE * LOCAL), jnp.float32)
        for member in range(MEMBERS):
            total = total + jnp.sum(jnp.exp2(scores(member, mine)), axis=0)
        store(step, shift + jnp.log2(jnp.sum(total, axis=0, keepdims=True)))

    def row_maximum(step, unused):
        mine = tile(step)
        highest = total = None
        for member in range(MEMBERS):
            score = scores(member, mine)
            top = jnp.max(score, axis=0)
            if member:
                top = jnp.maximum(top, highest)
            part = jnp.sum(jnp.exp2(score - top[None]), axis=0)
            total = part if member == 0 else part + total * jnp.exp2(highest - top)
            highest = top
        top = jnp.max(highest, axis=0, keepdims=True)
        total = jnp.sum(total * jnp.exp2(highest - top), axis=0, keepdims=True)
        store(step, top + jnp.log2(total))
        return unused

    @pl.when(near)
    def _():
        for step in range(MEMBERS // TILE):
            one_shift(step)

    @pl.when(jnp.logical_not(near))
    def _():
        lax.fori_loop(0, MEMBERS // TILE, row_maximum, 0)


def finish_kernel(place_ref, parts_ref, base_ref, potential_ref, new_ref, change_ref):
    parts = parts_ref[...]
    top = jnp.max(parts, axis=0)
    value = top + jnp.log2(jnp.sum(jnp.exp2(parts - top[None]), axis=0))
    change = base_ref[...] - (2.0 * LN2) * value
    row = lax.broadcasted_iota(jnp.int32, change.shape, 0)
    mine = jnp.sum(jnp.where(row == place_ref[0], change, 0.0), axis=0, keepdims=True)
    new_ref[...] = potential_ref[...] + 0.5 * mine
    whole = jnp.sum(jnp.sum(change * change, axis=0, keepdims=True), axis=1, keepdims=True)
    change_ref[...] = jnp.broadcast_to(whole, change_ref.shape)


def norm_kernel(count, parts_ref, out_ref):
    whole = jnp.sum(parts_ref[...], axis=0, keepdims=True)
    out_ref[...] = jnp.sqrt(whole / count + 1e-06)


def call(kernel, outs, *operands, limit=4, **options):
    return pl.pallas_call(
        kernel,
        out_shape=outs,
        compiler_params=pltpu.CompilerParams(vmem_limit_bytes=limit * MIB),
        **options,
    )(*operands)


IN_VMEM = pl.BlockSpec(memory_space=pltpu.VMEM)
IN_SMEM = pl.BlockSpec(memory_space=pltpu.SMEM)
ANYWHERE = pl.BlockSpec(memory_space=pl.ANY)


def shape(*dims, dtype=jnp.float32):
    return jax.ShapeDtypeStruct(dims, dtype)


def per_device(points, log_point_weight, potential):
    features = points.shape[1]
    narrow = lax.axis_size("narrow")
    core = lax.axis_index("narrow") % 2
    place = lax.axis_index("wide") % MEMBERS
    own_potential = potential.reshape(1, LOCAL)
    packed = call(
        pack_kernel,
        shape(LOCAL + TAIL, features, dtype=jnp.bfloat16),
        points,
        log_point_weight.reshape(1, LOCAL),
        own_potential,
        limit=60,
    )
    pair = lax.all_gather(
        packed,
        "narrow",
        axis=0,
        tiled=True,
        axis_index_groups=[[at, at + 1] for at in range(0, narrow, 2)],
    )
    message = call(
        spread_kernel, shape(MEMBERS, MESSAGE, features, dtype=jnp.bfloat16), pair, limit=8
    )
    own = lax.all_to_all(
        message,
        AXES,
        0,
        0,
        tiled=True,
        axis_index_groups=row_groups([0]) + column_groups([1]),
    )
    other = lax.ppermute(own, "narrow", [(at, at ^ 1) for at in range(narrow)])
    sums, base = call(
        pairs_kernel,
        (shape(MEMBERS, MEMBERS, LOCAL), shape(MEMBERS, LOCAL)),
        core.reshape(1),
        own,
        other,
        limit=24,
        in_specs=[IN_SMEM, ANYWHERE, ANYWHERE],
        out_specs=[IN_VMEM, IN_VMEM],
        scratch_shapes=[
            pltpu.VMEM((MEMBERS, LOCAL, features), jnp.bfloat16),
            pltpu.VMEM((MEMBERS, TAIL, features), jnp.bfloat16),
            pltpu.VMEM((MEMBERS, MESSAGE, features), jnp.bfloat16),
            pltpu.VMEM((MEMBERS, 2 * LOCAL, LOCAL), jnp.float32),
            pltpu.SemaphoreType.DMA((4,)),
        ],
    )
    parts = lax.all_to_all(
        sums,
        AXES,
        0,
        0,
        tiled=True,
        axis_index_groups=row_groups([0, 1]),
    )
    new_potential, change = call(
        finish_kernel,
        (shape(1, LOCAL), shape(2 * MEMBERS, LOCAL)),
        place.reshape(1),
        parts,
        base,
        own_potential,
        in_specs=[IN_SMEM, IN_VMEM, IN_VMEM, IN_VMEM],
        out_specs=[IN_VMEM, IN_VMEM],
    )
    changes = lax.all_to_all(
        change, AXES, 0, 0, tiled=True, axis_index_groups=remaining_groups()
    )
    count = LOCAL * lax.axis_size(AXES)
    norm = call(lambda a, b: norm_kernel(count, a, b), shape(1, LOCAL), changes)
    return new_potential.reshape(LOCAL), norm[0, 0]


def solution(mesh):
    in_specs = (P(AXES, None), P(AXES), P(AXES))
    out_specs = (P(AXES), P())
    return jax.shard_map(
        per_device, mesh=mesh, in_specs=in_specs, out_specs=out_specs, check_vma=False
    )
```

```python
import math

import jax
import jax.numpy as jnp
from jax import lax
from jax.experimental import pallas as pl
from jax.experimental.pallas import tpu as pltpu
from jax.sharding import PartitionSpec as P

LOG2E = math.log2(math.e)
LN2 = math.log(2.0)
AXES = ("wide", "narrow")
SHAPE = (2, 4, 8, 4, 2)
MEMBERS = 16
LOCAL = 128
TAIL = 16
TILE = 4
MESSAGE = 2 * LOCAL + TAIL
MIB = 1024 * 1024
PAIRS = ((0, 1), (2, 3))
CROSS = ((1, 2), (3, 0))


def index(x, y, z, core):
    where = 0
    for size, at in zip(SHAPE, (z % 2, x, y, z // 2, core)):
        where = where * size + at
    return where


def row_groups(cores):
    return [
        [index(x, y, z, core) for x in pair for y in range(8)]
        for pair in PAIRS
        for z in range(8)
        for core in cores
    ]


def column_groups(cores):
    return [
        [index(x, y, z, core) for x in pair for z in range(8)]
        for pair in CROSS
        for y in range(8)
        for core in cores
    ]


def remaining_groups():
    return [
        [index(x, y, z, core) for x in pair for z in range(8) for core in range(2)]
        for pair in CROSS
        for y in range(8)
    ]


def three_terms(value):
    high = value.astype(jnp.bfloat16).astype(jnp.float32)
    rest = value - high
    middle = rest.astype(jnp.bfloat16).astype(jnp.float32)
    return high, middle, rest - middle


def pack_kernel(points_ref, weight_ref, potential_ref, out_ref):
    points = points_ref[...]
    wide = points.astype(jnp.float32)
    square = wide * wide
    high = square.astype(jnp.bfloat16)
    low = (square - high.astype(jnp.float32)).astype(jnp.bfloat16)
    ones = jnp.ones((8, points.shape[1]), jnp.bfloat16)
    dims = (((1,), (1,)), ((), ()))
    norms = lax.dot_general(ones, high, dims, preferred_element_type=jnp.float32)
    norms = norms + lax.dot_general(ones, low, dims, preferred_element_type=jnp.float32)
    norms = norms[:1]
    potential = potential_ref[...]
    mass = weight_ref[...] + 0.5 * potential
    offset = (mass - 0.25 * norms) * LOG2E
    own_term = (mass + 0.25 * norms) * LOG2E
    left = three_terms(offset) + three_terms(mass * LOG2E)
    right = three_terms(0.5 * norms - potential) + three_terms(own_term)
    rows = [jnp.concatenate(both, axis=1) for both in zip(left, right)]
    half = jnp.concatenate(rows + [jnp.zeros((2, 2 * LOCAL), jnp.float32)], axis=0)
    out_ref[:LOCAL] = points
    out_ref[LOCAL:] = jnp.concatenate([half, half], axis=0).astype(jnp.bfloat16)


def spread_kernel(pair_ref, out_ref):
    stride = LOCAL + TAIL
    first, second = pair_ref[LOCAL:stride], pair_ref[stride + LOCAL :]
    row = lax.broadcasted_iota(jnp.int32, first.shape, 0)
    tail = jnp.where(row < 8, first.astype(jnp.float32), second.astype(jnp.float32))
    tail = tail.astype(jnp.bfloat16)
    for member in range(MEMBERS):
        out_ref[member, :LOCAL] = pair_ref[:LOCAL]
        out_ref[member, LOCAL : 2 * LOCAL] = pair_ref[stride : stride + LOCAL]
        out_ref[member, 2 * LOCAL :] = tail


def pairs_kernel(
    own_ref, other_ref, sum_ref, base_ref, rows, row_tail, columns, offsets, sems
):
    core = lax.axis_index("narrow") & 1

    def copies(row_source, column_source):
        mine = pl.ds(pl.multiple_of(core * LOCAL, LOCAL), LOCAL)
        points, tail = pl.ds(0, 2 * LOCAL), pl.ds(2 * LOCAL, TAIL)
        plan = [
            (row_source.at[:, tail], row_tail),
            (column_source.at[:, tail], columns.at[:, tail]),
            (row_source.at[:, mine], rows),
            (column_source.at[:, points], columns.at[:, points]),
        ]
        return [
            pltpu.make_async_copy(source, target, sems.at[at])
            for at, (source, target) in enumerate(plan)
        ]

    @pl.when(core == 0)
    def _():
        for copy in copies(own_ref, other_ref):
            copy.start()

    @pl.when(core == 1)
    def _():
        for copy in copies(other_ref, own_ref):
            copy.start()

    waits = copies(own_ref, other_ref)
    waits[0].wait()
    waits[1].wait()

    half = lax.broadcasted_iota(jnp.int32, (MEMBERS, 8, LOCAL), 1)

    def gather(tail, first):
        pick = (half >= first) & (half < first + 3)
        return jnp.sum(jnp.where(pick, tail, 0.0), axis=1)

    tails = row_tail[...].astype(jnp.float32)
    tails = jnp.where(core == 0, tails[:, :8], tails[:, 8:])
    base_ref[...] = gather(tails[:, :, LOCAL:], 0)
    own_term = gather(tails[:, :, LOCAL:], 3)
    least = jnp.min(own_term)
    quarter = jnp.max(own_term - gather(tails[:, :, :LOCAL], 3))
    tails = columns[:, 2 * LOCAL :, :LOCAL].astype(jnp.float32)
    mass = jnp.max(jnp.maximum(gather(tails[:, :8], 3), gather(tails[:, 8:], 3)))
    near = mass + quarter - least <= 200.0
    shift = jnp.where(near, least + 90.0, 0.0)

    row = lax.broadcasted_iota(jnp.int32, (TAIL, LOCAL), 0)
    for member in range(MEMBERS):
        tail = columns[member, 2 * LOCAL :, :LOCAL]
        for side in range(2):
            pick = (row >= 8 * side) & (row < 8 * side + 3)
            offsets[member, side * LOCAL : (side + 1) * LOCAL] = lax.dot_general(
                tail,
                jnp.where(pick, 1.0, 0.0).astype(jnp.bfloat16),
                (((0,), (0,)), ((), ())),
                preferred_element_type=jnp.float32,
            ) - shift

    waits[2].wait()
    waits[3].wait()

    def scores(member, mine):
        inner = lax.dot_general(
            columns[member, : 2 * LOCAL],
            mine,
            (((1,), (1,)), ((), ())),
            preferred_element_type=jnp.float32,
        )
        score = inner * (0.5 * LOG2E) + jnp.concatenate([offsets[member]] * TILE, axis=1)
        return score.reshape(2 * LOCAL // 8, 8, TILE * LOCAL)

    def store(step, value):
        for block in range(TILE):
            line = value[:, block * LOCAL : (block + 1) * LOCAL]
            for member in range(MEMBERS):
                sum_ref[member, pl.ds(step * TILE + block, 1)] = line

    def tile(step):
        return rows[pl.ds(step * TILE, TILE)].reshape(TILE * LOCAL, -1)

    def one_shift(step):
        mine = tile(step)
        total = jnp.zeros((8, TILE * LOCAL), jnp.float32)
        for member in range(MEMBERS):
            total = total + jnp.sum(jnp.exp2(scores(member, mine)), axis=0)
        store(step, shift + jnp.log2(jnp.sum(total, axis=0, keepdims=True)))

    def row_maximum(step, unused):
        mine = tile(step)
        highest = total = None
        for member in range(MEMBERS):
            score = scores(member, mine)
            top = jnp.max(score, axis=0)
            if member:
                top = jnp.maximum(top, highest)
            part = jnp.sum(jnp.exp2(score - top[None]), axis=0)
            total = part if member == 0 else part + total * jnp.exp2(highest - top)
            highest = top
        top = jnp.max(highest, axis=0, keepdims=True)
        total = jnp.sum(total * jnp.exp2(highest - top), axis=0, keepdims=True)
        store(step, top + jnp.log2(total))
        return unused

    @pl.when(near)
    def _():
        for step in range(MEMBERS // TILE):
            one_shift(step)

    @pl.when(jnp.logical_not(near))
    def _():
        lax.fori_loop(0, MEMBERS // TILE, row_maximum, 0)


def finish_kernel(parts_ref, base_ref, potential_ref, new_ref, change_ref):
    parts = parts_ref[...]
    top = jnp.max(parts, axis=0)
    value = top + jnp.log2(jnp.sum(jnp.exp2(parts - top[None]), axis=0))
    change = base_ref[...] - (2.0 * LN2) * value
    row = lax.broadcasted_iota(jnp.int32, change.shape, 0)
    mine = jnp.sum(jnp.where(row == lax.axis_index("wide") & (MEMBERS - 1), change, 0.0), axis=0, keepdims=True)
    new_ref[...] = potential_ref[...] + 0.5 * mine
    whole = jnp.sum(jnp.sum(change * change, axis=0, keepdims=True), axis=1, keepdims=True)
    change_ref[...] = jnp.broadcast_to(whole, change_ref.shape)


def norm_kernel(count, parts_ref, out_ref):
    whole = jnp.sum(parts_ref[...], axis=0, keepdims=True)
    out_ref[...] = jnp.sqrt(whole / count + 1e-06)


def call(kernel, outs, *operands, limit=4, **options):
    return pl.pallas_call(
        kernel,
        out_shape=outs,
        compiler_params=pltpu.CompilerParams(vmem_limit_bytes=limit * MIB),
        **options,
    )(*operands)


IN_VMEM = pl.BlockSpec(memory_space=pltpu.VMEM)
ANYWHERE = pl.BlockSpec(memory_space=pl.ANY)


def shape(*dims, dtype=jnp.float32):
    return jax.ShapeDtypeStruct(dims, dtype)


def per_device(points, log_point_weight, potential):
    features = points.shape[1]
    narrow = lax.axis_size("narrow")
    own_potential = potential.reshape(1, LOCAL)
    packed = call(
        pack_kernel,
        shape(LOCAL + TAIL, features, dtype=jnp.bfloat16),
        points,
        log_point_weight.reshape(1, LOCAL),
        own_potential,
        limit=60,
    )
    pair = lax.all_gather(
        packed,
        "narrow",
        axis=0,
        tiled=True,
        axis_index_groups=[[at, at + 1] for at in range(0, narrow, 2)],
    )
    message = call(
        spread_kernel, shape(MEMBERS, MESSAGE, features, dtype=jnp.bfloat16), pair, limit=8
    )
    own = lax.all_to_all(
        message,
        AXES,
        0,
        0,
        tiled=True,
        axis_index_groups=row_groups([0]) + column_groups([1]),
    )
    other = lax.ppermute(own, "narrow", [(at, at ^ 1) for at in range(narrow)])
    sums, base = call(
        pairs_kernel,
        (shape(MEMBERS, MEMBERS, LOCAL), shape(MEMBERS, LOCAL)),
        own,
        other,
        limit=16,
        in_specs=[ANYWHERE, ANYWHERE],
        out_specs=[IN_VMEM, IN_VMEM],
        scratch_shapes=[
            pltpu.VMEM((MEMBERS, LOCAL, features), jnp.bfloat16),
            pltpu.VMEM((MEMBERS, TAIL, features), jnp.bfloat16),
            pltpu.VMEM((MEMBERS, MESSAGE, features), jnp.bfloat16),
            pltpu.VMEM((MEMBERS, 2 * LOCAL, LOCAL), jnp.float32),
            pltpu.SemaphoreType.DMA((4,)),
        ],
    )
    parts = lax.all_to_all(
        sums,
        AXES,
        0,
        0,
        tiled=True,
        axis_index_groups=row_groups([0, 1]),
    )
    new_potential, change = call(
        finish_kernel,
        (shape(1, LOCAL), shape(2 * MEMBERS, LOCAL)),
        parts,
        base,
        own_potential,
        in_specs=[IN_VMEM, IN_VMEM, IN_VMEM],
        out_specs=[IN_VMEM, IN_VMEM],
    )
    changes = lax.all_to_all(
        change, AXES, 0, 0, tiled=True, axis_index_groups=remaining_groups()
    )
    count = LOCAL * lax.axis_size(AXES)
    norm = call(lambda a, b: norm_kernel(count, a, b), shape(1, LOCAL), changes)
    return new_potential.reshape(LOCAL), norm[0, 0]


def solution(mesh):
    in_specs = (P(AXES, None), P(AXES), P(AXES))
    out_specs = (P(AXES), P())
    return jax.shard_map(
        per_device, mesh=mesh, in_specs=in_specs, out_specs=out_specs, check_vma=False
    )
```

```python
import functools
import math

import jax
import jax.numpy as jnp
from jax import lax
from jax.experimental import pallas as pl
from jax.experimental.pallas import tpu as pltpu
from jax.sharding import PartitionSpec as P

LOG2E = math.log2(math.e)
LN2 = math.log(2.0)
AXES = ("wide", "narrow")
SHAPE = (2, 4, 8, 4, 2)
MEMBERS = 16
LOCAL = 128
TAIL = 16
TILE = 4
MESSAGE = 2 * LOCAL + TAIL
MIB = 1024 * 1024
PAIRS = ((0, 1), (2, 3))
CROSS = ((1, 2), (3, 0))


def index(x, y, z, core):
    where = 0
    for size, at in zip(SHAPE, (z % 2, x, y, z // 2, core)):
        where = where * size + at
    return where


def row_groups(cores):
    return [
        [index(x, y, z, core) for x in pair for y in range(8)]
        for pair in PAIRS
        for z in range(8)
        for core in cores
    ]


def column_groups(cores):
    return [
        [index(x, y, z, core) for x in pair for z in range(8)]
        for pair in CROSS
        for y in range(8)
        for core in cores
    ]


def remaining_groups():
    return [
        [index(x, y, z, core) for x in pair for z in range(8) for core in range(2)]
        for pair in CROSS
        for y in range(8)
    ]


def three_terms(value):
    high = value.astype(jnp.bfloat16).astype(jnp.float32)
    rest = value - high
    middle = rest.astype(jnp.bfloat16).astype(jnp.float32)
    return high, middle, rest - middle


def pack_kernel(points_ref, weight_ref, potential_ref, out_ref):
    points = points_ref[...]
    wide = points.astype(jnp.float32)
    square = wide * wide
    high = square.astype(jnp.bfloat16)
    low = (square - high.astype(jnp.float32)).astype(jnp.bfloat16)
    ones = jnp.ones((8, points.shape[1]), jnp.bfloat16)
    dims = (((1,), (1,)), ((), ()))
    norms = lax.dot_general(ones, high, dims, preferred_element_type=jnp.float32)
    norms = norms + lax.dot_general(ones, low, dims, preferred_element_type=jnp.float32)
    norms = norms[:1]
    potential = potential_ref[...]
    mass = weight_ref[...] + 0.5 * potential
    offset = (mass - 0.25 * norms) * LOG2E
    own_term = (mass + 0.25 * norms) * LOG2E
    left = three_terms(offset) + three_terms(mass * LOG2E)
    right = three_terms(0.5 * norms - potential) + three_terms(own_term)
    rows = [jnp.concatenate(both, axis=1) for both in zip(left, right)]
    half = jnp.concatenate(rows + [jnp.zeros((2, 2 * LOCAL), jnp.float32)], axis=0)
    out_ref[:LOCAL] = points
    out_ref[LOCAL:] = jnp.concatenate([half, half], axis=0).astype(jnp.bfloat16)


def spread_kernel(pair_ref, out_ref):
    stride = LOCAL + TAIL
    first, second = pair_ref[LOCAL:stride], pair_ref[stride + LOCAL :]
    row = lax.broadcasted_iota(jnp.int32, first.shape, 0)
    tail = jnp.where(row < 8, first.astype(jnp.float32), second.astype(jnp.float32))
    tail = tail.astype(jnp.bfloat16)
    for member in range(MEMBERS):
        out_ref[member, :LOCAL] = pair_ref[:LOCAL]
        out_ref[member, LOCAL : 2 * LOCAL] = pair_ref[stride : stride + LOCAL]
        out_ref[member, 2 * LOCAL :] = tail


def log_sums(row_ref, column_ref, core, offsets):
    line = lax.broadcasted_iota(jnp.int32, (1, 8, LOCAL), 1)

    def gather(tail, first):
        pick = (line >= first) & (line < first + 3)
        return jnp.sum(jnp.where(pick, tail, 0.0), axis=1)

    own = slice(2 * LOCAL, MESSAGE)
    tails = row_ref[:, own].astype(jnp.float32)[:, 8 * core : 8 * core + 8]
    base = gather(tails[:, :, LOCAL:], 0)
    own_term = gather(tails[:, :, LOCAL:], 3)
    least = jnp.min(own_term)
    quarter = jnp.max(own_term - gather(tails[:, :, :LOCAL], 3))
    tails = column_ref[:, own, :LOCAL].astype(jnp.float32)
    mass = jnp.max(jnp.maximum(gather(tails[:, :8], 3), gather(tails[:, 8:], 3)))
    near = mass + quarter - least <= 200.0
    shift = jnp.where(near, least + 90.0, 0.0)

    row = lax.broadcasted_iota(jnp.int32, (TAIL, LOCAL), 0)
    columns = column_ref.shape[0]
    for block in range(columns):
        for side in range(2):
            pick = (row >= 8 * side) & (row < 8 * side + 3)
            offsets[block, side * LOCAL : (side + 1) * LOCAL] = lax.dot_general(
                column_ref[block, own, :LOCAL],
                jnp.where(pick, 1.0, 0.0).astype(jnp.bfloat16),
                (((0,), (0,)), ((), ())),
                preferred_element_type=jnp.float32,
            ) - shift

    def scores(block, mine):
        inner = lax.dot_general(
            column_ref[block, : 2 * LOCAL],
            mine,
            (((1,), (1,)), ((), ())),
            preferred_element_type=jnp.float32,
        )
        score = inner * (0.5 * LOG2E) + jnp.concatenate([offsets[block]] * TILE, axis=1)
        return score.reshape(2 * LOCAL // 8, 8, TILE * LOCAL)

    def one_shift(mine):
        total = jnp.zeros((8, TILE * LOCAL), jnp.float32)
        for block in range(columns):
            total = total + jnp.sum(jnp.exp2(scores(block, mine)), axis=0)
        total = jnp.maximum(jnp.sum(total, axis=0, keepdims=True), 2.0**-126)
        return shift + jnp.log2(total)

    def row_maximum(mine):
        def step(block, carry):
            highest, total = carry
            score = scores(block, mine)
            top = jnp.maximum(highest, jnp.max(score, axis=0))
            total = total * jnp.exp2(highest - top) + jnp.sum(jnp.exp2(score - top[None]), axis=0)
            return top, total

        start = jnp.full((8, TILE * LOCAL), -1e30, jnp.float32)
        highest, total = lax.fori_loop(0, columns, step, (start, jnp.zeros_like(start)))
        top = jnp.max(highest, axis=0, keepdims=True)
        total = jnp.sum(total * jnp.exp2(highest - top), axis=0, keepdims=True)
        return top + jnp.log2(total)

    def run(method):
        lines = []
        for step in range(0, row_ref.shape[0], TILE):
            mine = row_ref[step : step + TILE, core * LOCAL : (core + 1) * LOCAL]
            value = method(mine.reshape(TILE * LOCAL, -1))
            lines += [value[:, at * LOCAL : (at + 1) * LOCAL] for at in range(TILE)]
        return jnp.concatenate(lines, axis=0)

    return lax.cond(near, lambda: run(one_shift), lambda: run(row_maximum)), base


def pairs_kernel(final, own_ref, part_ref, *refs):
    if final:
        sum_before, base_before, sum_ref, base_ref, offsets = refs
    else:
        sum_ref, base_ref, offsets = refs
    where = lax.axis_index("narrow") & 1
    half = MEMBERS // 2

    def store(value, base):
        base_ref[...] = base
        if not final:
            sum_ref[...] = value
            return
        before = sum_before[...]
        top = jnp.maximum(before, value)
        value = top + jnp.log2(jnp.exp2(before - top) + jnp.exp2(value - top))
        for member in range(MEMBERS):
            sum_ref[member] = value

    @pl.when(where == 0)
    def _():
        store(*log_sums(own_ref, part_ref, 0, offsets))

    @pl.when(where == 1)
    def _():
        value, base = log_sums(part_ref, own_ref, 1, offsets)
        missing = jnp.full(value.shape, -1e30, jnp.float32)
        if final:
            store(
                jnp.concatenate([missing, value], axis=0),
                jnp.concatenate([base_before[:half], base], axis=0),
            )
        else:
            store(
                jnp.concatenate([value, missing], axis=0),
                jnp.concatenate([base, base], axis=0),
            )


def finish_kernel(parts_ref, base_ref, potential_ref, new_ref, change_ref):
    parts = parts_ref[...]
    top = jnp.max(parts, axis=0)
    value = top + jnp.log2(jnp.sum(jnp.exp2(parts - top[None]), axis=0))
    change = base_ref[...] - (2.0 * LN2) * value
    row = lax.broadcasted_iota(jnp.int32, change.shape, 0)
    mine = jnp.sum(jnp.where(row == lax.axis_index("wide") & (MEMBERS - 1), change, 0.0), axis=0, keepdims=True)
    new_ref[...] = potential_ref[...] + 0.5 * mine
    whole = jnp.sum(jnp.sum(change * change, axis=0, keepdims=True), axis=1, keepdims=True)
    change_ref[...] = jnp.broadcast_to(whole, change_ref.shape)


def norm_kernel(count, parts_ref, out_ref):
    whole = jnp.sum(parts_ref[...], axis=0, keepdims=True)
    out_ref[...] = jnp.sqrt(whole / count + 1e-06)


def call(kernel, outs, *operands, limit=4, **options):
    return pl.pallas_call(
        kernel,
        out_shape=outs,
        compiler_params=pltpu.CompilerParams(vmem_limit_bytes=limit * MIB),
        **options,
    )(*operands)


IN_VMEM = pl.BlockSpec(memory_space=pltpu.VMEM)


def shape(*dims, dtype=jnp.float32):
    return jax.ShapeDtypeStruct(dims, dtype)


def per_device(points, log_point_weight, potential):
    features = points.shape[1]
    narrow = lax.axis_size("narrow")
    own_potential = potential.reshape(1, LOCAL)
    packed = call(
        pack_kernel,
        shape(LOCAL + TAIL, features, dtype=jnp.bfloat16),
        points,
        log_point_weight.reshape(1, LOCAL),
        own_potential,
        limit=60,
    )
    pair = lax.all_gather(
        packed,
        "narrow",
        axis=0,
        tiled=True,
        axis_index_groups=[[at, at + 1] for at in range(0, narrow, 2)],
    )
    message = call(
        spread_kernel, shape(MEMBERS, MESSAGE, features, dtype=jnp.bfloat16), pair, limit=8
    )
    own = lax.all_to_all(
        message,
        AXES,
        0,
        0,
        tiled=True,
        axis_index_groups=row_groups([0]) + column_groups([1]),
    )
    other_core = [(at, at ^ 1) for at in range(narrow)]
    halves = [lax.ppermute(part, "narrow", other_core) for part in jnp.split(own, 2)]
    offsets = [pltpu.VMEM((MEMBERS, 2 * LOCAL, LOCAL), jnp.float32)]
    lines = shape(MEMBERS, LOCAL)
    before = call(
        functools.partial(pairs_kernel, False),
        (lines, lines),
        own,
        halves[0],
        limit=10,
        scratch_shapes=offsets,
    )
    sums, base = call(
        functools.partial(pairs_kernel, True),
        (shape(MEMBERS, MEMBERS, LOCAL), lines),
        own,
        halves[1],
        *before,
        limit=10,
        scratch_shapes=offsets,
    )
    parts = lax.all_to_all(
        sums,
        AXES,
        0,
        0,
        tiled=True,
        axis_index_groups=row_groups([0, 1]),
    )
    new_potential, change = call(
        finish_kernel,
        (shape(1, LOCAL), shape(2 * MEMBERS, LOCAL)),
        parts,
        base,
        own_potential,
        in_specs=[IN_VMEM, IN_VMEM, IN_VMEM],
        out_specs=[IN_VMEM, IN_VMEM],
    )
    changes = lax.all_to_all(
        change, AXES, 0, 0, tiled=True, axis_index_groups=remaining_groups()
    )
    count = LOCAL * lax.axis_size(AXES)
    norm = call(lambda a, b: norm_kernel(count, a, b), shape(1, LOCAL), changes)
    return new_potential.reshape(LOCAL), norm[0, 0]


def solution(mesh):
    in_specs = (P(AXES, None), P(AXES), P(AXES))
    out_specs = (P(AXES), P())
    return jax.shard_map(
        per_device, mesh=mesh, in_specs=in_specs, out_specs=out_specs, check_vma=False
    )
```

```python
import functools
import math

import jax
import jax.numpy as jnp
from jax import lax
from jax.experimental import pallas as pl
from jax.experimental.pallas import tpu as pltpu
from jax.sharding import PartitionSpec as P

LOG2E = math.log2(math.e)
LN2 = math.log(2.0)
AXES = ("wide", "narrow")
SHAPE = (2, 4, 8, 4, 2)
MEMBERS = 16
LOCAL = 128
TAIL = 16
TILE = 4
MESSAGE = 2 * LOCAL + TAIL
MIB = 1024 * 1024
PAIRS = ((0, 1), (2, 3))
CROSS = ((1, 2), (3, 0))


def index(x, y, z, core):
    where = 0
    for size, at in zip(SHAPE, (z % 2, x, y, z // 2, core)):
        where = where * size + at
    return where


def row_groups(cores):
    return [
        [index(x, y, z, core) for x in pair for y in range(8)]
        for pair in PAIRS
        for z in range(8)
        for core in cores
    ]


def column_groups(cores):
    return [
        [index(x, y, z, core) for x in pair for z in range(8)]
        for pair in CROSS
        for y in range(8)
        for core in cores
    ]


def remaining_groups():
    return [
        [index(x, y, z, core) for x in pair for z in range(8) for core in range(2)]
        for pair in CROSS
        for y in range(8)
    ]


def three_terms(value):
    high = value.astype(jnp.bfloat16).astype(jnp.float32)
    rest = value - high
    middle = rest.astype(jnp.bfloat16).astype(jnp.float32)
    return high, middle, rest - middle


def pack_kernel(points_ref, weight_ref, potential_ref, out_ref):
    points = points_ref[...]
    wide = points.astype(jnp.float32)
    square = wide * wide
    high = square.astype(jnp.bfloat16)
    low = (square - high.astype(jnp.float32)).astype(jnp.bfloat16)
    ones = jnp.ones((8, points.shape[1]), jnp.bfloat16)
    dims = (((1,), (1,)), ((), ()))
    norms = lax.dot_general(ones, high, dims, preferred_element_type=jnp.float32)
    norms = norms + lax.dot_general(ones, low, dims, preferred_element_type=jnp.float32)
    norms = norms[:1]
    potential = potential_ref[...]
    mass = weight_ref[...] + 0.5 * potential
    offset = (mass - 0.25 * norms) * LOG2E
    own_term = (mass + 0.25 * norms) * LOG2E
    left = three_terms(offset) + three_terms(mass * LOG2E)
    right = three_terms(0.5 * norms - potential) + three_terms(own_term)
    rows = [jnp.concatenate(both, axis=1) for both in zip(left, right)]
    half = jnp.concatenate(rows + [jnp.zeros((2, 2 * LOCAL), jnp.float32)], axis=0)
    out_ref[:LOCAL] = points
    out_ref[LOCAL:] = jnp.concatenate([half, half], axis=0).astype(jnp.bfloat16)


def spread_kernel(pair_ref, out_ref):
    stride = LOCAL + TAIL
    first, second = pair_ref[LOCAL:stride], pair_ref[stride + LOCAL :]
    row = lax.broadcasted_iota(jnp.int32, first.shape, 0)
    tail = jnp.where(row < 8, first.astype(jnp.float32), second.astype(jnp.float32))
    tail = tail.astype(jnp.bfloat16)
    for member in range(MEMBERS):
        out_ref[member, :LOCAL] = pair_ref[:LOCAL]
        out_ref[member, LOCAL : 2 * LOCAL] = pair_ref[stride : stride + LOCAL]
        out_ref[member, 2 * LOCAL :] = tail


def log_sums(row_ref, column_ref, core, offsets):
    line = lax.broadcasted_iota(jnp.int32, (1, 8, LOCAL), 1)

    def gather(tail, first):
        pick = (line >= first) & (line < first + 3)
        return jnp.sum(jnp.where(pick, tail, 0.0), axis=1)

    own = slice(2 * LOCAL, MESSAGE)
    tails = row_ref[:, own].astype(jnp.float32)[:, 8 * core : 8 * core + 8]
    base = gather(tails[:, :, LOCAL:], 0)
    own_term = gather(tails[:, :, LOCAL:], 3)
    least = jnp.min(own_term)
    quarter = jnp.max(own_term - gather(tails[:, :, :LOCAL], 3))
    tails = column_ref[:, own, :LOCAL].astype(jnp.float32)
    mass = jnp.max(jnp.maximum(gather(tails[:, :8], 3), gather(tails[:, 8:], 3)))
    near = mass + quarter - least <= 200.0
    shift = jnp.where(near, least + 90.0, 0.0)

    row = lax.broadcasted_iota(jnp.int32, (TAIL, 2 * LOCAL), 0)
    start = lax.broadcasted_iota(jnp.int32, (TAIL, 2 * LOCAL), 1) // LOCAL * 8
    pick = jnp.where((row >= start) & (row < start + 3), 1.0, 0.0).astype(jnp.bfloat16)
    columns = column_ref.shape[0]
    for block in range(columns):
        both = lax.dot_general(
            column_ref[block, own, :LOCAL],
            pick,
            (((0,), (0,)), ((), ())),
            preferred_element_type=jnp.float32,
        ) - shift
        offsets[block, :LOCAL] = both[:, :LOCAL]
        offsets[block, LOCAL:] = both[:, LOCAL:]

    def scores(block, mine):
        inner = lax.dot_general(
            column_ref[block, : 2 * LOCAL],
            mine,
            (((1,), (1,)), ((), ())),
            preferred_element_type=jnp.float32,
        )
        score = inner * (0.5 * LOG2E) + jnp.concatenate([offsets[block]] * TILE, axis=1)
        return score.reshape(2 * LOCAL // 8, 8, TILE * LOCAL)

    def one_shift(mine):
        total = jnp.zeros((8, TILE * LOCAL), jnp.float32)
        for block in range(columns):
            total = total + jnp.sum(jnp.exp2(scores(block, mine)), axis=0)
        total = jnp.maximum(jnp.sum(total, axis=0, keepdims=True), 2.0**-126)
        return shift + jnp.log2(total)

    def row_maximum(mine):
        def step(block, carry):
            highest, total = carry
            score = scores(block, mine)
            top = jnp.maximum(highest, jnp.max(score, axis=0))
            total = total * jnp.exp2(highest - top) + jnp.sum(jnp.exp2(score - top[None]), axis=0)
            return top, total

        start = jnp.full((8, TILE * LOCAL), -1e30, jnp.float32)
        highest, total = lax.fori_loop(0, columns, step, (start, jnp.zeros_like(start)))
        top = jnp.max(highest, axis=0, keepdims=True)
        total = jnp.sum(total * jnp.exp2(highest - top), axis=0, keepdims=True)
        return top + jnp.log2(total)

    def run(method):
        lines = []
        for step in range(0, row_ref.shape[0], TILE):
            mine = row_ref[step : step + TILE, core * LOCAL : (core + 1) * LOCAL]
            value = method(mine.reshape(TILE * LOCAL, -1))
            lines += [value[:, at * LOCAL : (at + 1) * LOCAL] for at in range(TILE)]
        return jnp.concatenate(lines, axis=0)

    return lax.cond(near, lambda: run(one_shift), lambda: run(row_maximum)), base


def pairs_kernel(final, own_ref, part_ref, *refs):
    if final:
        sum_before, base_before, sum_ref, base_ref, offsets = refs
    else:
        sum_ref, base_ref, offsets = refs
    where = lax.axis_index("narrow") & 1
    half = MEMBERS // 2

    def store(value, base):
        base_ref[...] = base
        if not final:
            sum_ref[...] = value
            return
        before = sum_before[...]
        top = jnp.maximum(before, value)
        value = top + jnp.log2(jnp.exp2(before - top) + jnp.exp2(value - top))
        for member in range(MEMBERS):
            sum_ref[member] = value

    @pl.when(where == 0)
    def _():
        store(*log_sums(own_ref, part_ref, 0, offsets))

    @pl.when(where == 1)
    def _():
        value, base = log_sums(part_ref, own_ref, 1, offsets)
        missing = jnp.full(value.shape, -1e30, jnp.float32)
        if final:
            store(
                jnp.concatenate([missing, value], axis=0),
                jnp.concatenate([base_before[:half], base], axis=0),
            )
        else:
            store(
                jnp.concatenate([value, missing], axis=0),
                jnp.concatenate([base, base], axis=0),
            )


def finish_kernel(parts_ref, base_ref, potential_ref, new_ref, change_ref):
    parts = parts_ref[...]
    top = jnp.max(parts, axis=0)
    value = top + jnp.log2(jnp.sum(jnp.exp2(parts - top[None]), axis=0))
    change = base_ref[...] - (2.0 * LN2) * value
    row = lax.broadcasted_iota(jnp.int32, change.shape, 0)
    mine = jnp.sum(jnp.where(row == lax.axis_index("wide") & (MEMBERS - 1), change, 0.0), axis=0, keepdims=True)
    new_ref[...] = potential_ref[...] + 0.5 * mine
    whole = jnp.sum(jnp.sum(change * change, axis=0, keepdims=True), axis=1, keepdims=True)
    change_ref[...] = jnp.broadcast_to(whole, change_ref.shape)


def norm_kernel(count, parts_ref, out_ref):
    whole = jnp.sum(parts_ref[...], axis=0, keepdims=True)
    out_ref[...] = jnp.sqrt(whole / count + 1e-06)


def call(kernel, outs, *operands, limit=4, **options):
    return pl.pallas_call(
        kernel,
        out_shape=outs,
        compiler_params=pltpu.CompilerParams(vmem_limit_bytes=limit * MIB),
        **options,
    )(*operands)


IN_VMEM = pl.BlockSpec(memory_space=pltpu.VMEM)


def shape(*dims, dtype=jnp.float32):
    return jax.ShapeDtypeStruct(dims, dtype)


def per_device(points, log_point_weight, potential):
    features = points.shape[1]
    narrow = lax.axis_size("narrow")
    own_potential = potential.reshape(1, LOCAL)
    packed = call(
        pack_kernel,
        shape(LOCAL + TAIL, features, dtype=jnp.bfloat16),
        points,
        log_point_weight.reshape(1, LOCAL),
        own_potential,
        limit=60,
    )
    pair = lax.all_gather(
        packed,
        "narrow",
        axis=0,
        tiled=True,
        axis_index_groups=[[at, at + 1] for at in range(0, narrow, 2)],
    )
    message = call(
        spread_kernel, shape(MEMBERS, MESSAGE, features, dtype=jnp.bfloat16), pair, limit=8
    )
    own = lax.all_to_all(
        message,
        AXES,
        0,
        0,
        tiled=True,
        axis_index_groups=row_groups([0]) + column_groups([1]),
    )
    other_core = [(at, at ^ 1) for at in range(narrow)]
    halves = [lax.ppermute(part, "narrow", other_core) for part in jnp.split(own, 2)]
    offsets = [pltpu.VMEM((MEMBERS, 2 * LOCAL, LOCAL), jnp.float32)]
    lines = shape(MEMBERS, LOCAL)
    before = call(
        functools.partial(pairs_kernel, False),
        (lines, lines),
        own,
        halves[0],
        limit=10,
        scratch_shapes=offsets,
    )
    sums, base = call(
        functools.partial(pairs_kernel, True),
        (shape(MEMBERS, MEMBERS, LOCAL), lines),
        own,
        halves[1],
        *before,
        limit=10,
        scratch_shapes=offsets,
    )
    parts = lax.all_to_all(
        sums,
        AXES,
        0,
        0,
        tiled=True,
        axis_index_groups=row_groups([0, 1]),
    )
    new_potential, change = call(
        finish_kernel,
        (shape(1, LOCAL), shape(2 * MEMBERS, LOCAL)),
        parts,
        base,
        own_potential,
        in_specs=[IN_VMEM, IN_VMEM, IN_VMEM],
        out_specs=[IN_VMEM, IN_VMEM],
    )
    changes = lax.all_to_all(
        change, AXES, 0, 0, tiled=True, axis_index_groups=remaining_groups()
    )
    count = LOCAL * lax.axis_size(AXES)
    norm = call(lambda a, b: norm_kernel(count, a, b), shape(1, LOCAL), changes)
    return new_potential.reshape(LOCAL), norm[0, 0]


def solution(mesh):
    in_specs = (P(AXES, None), P(AXES), P(AXES))
    out_specs = (P(AXES), P())
    return jax.shard_map(
        per_device, mesh=mesh, in_specs=in_specs, out_specs=out_specs, check_vma=False
    )
```

```python
import functools
import math

import jax
import jax.numpy as jnp
from jax import lax
from jax.experimental import pallas as pl
from jax.experimental.pallas import tpu as pltpu
from jax.sharding import PartitionSpec as P

LOG2E = math.log2(math.e)
LN2 = math.log(2.0)
AXES = ("wide", "narrow")
SHAPE = (2, 4, 8, 4, 2)
MEMBERS = 16
LOCAL = 128
TAIL = 16
TILE = 2
MESSAGE = 2 * LOCAL + TAIL
FIRST = 6
MIB = 1024 * 1024
PAIRS = ((0, 1), (2, 3))
CROSS = ((1, 2), (3, 0))


def index(x, y, z, core):
    where = 0
    for size, at in zip(SHAPE, (z % 2, x, y, z // 2, core)):
        where = where * size + at
    return where


def row_groups(cores):
    return [
        [index(x, y, z, core) for x in pair for y in range(8)]
        for pair in PAIRS
        for z in range(8)
        for core in cores
    ]


def column_groups(cores):
    return [
        [index(x, y, z, core) for x in pair for z in range(8)]
        for pair in CROSS
        for y in range(8)
        for core in cores
    ]


def remaining_groups():
    return [
        [index(x, y, z, core) for x in pair for z in range(8) for core in range(2)]
        for pair in CROSS
        for y in range(8)
    ]


def three_terms(value):
    high = value.astype(jnp.bfloat16).astype(jnp.float32)
    rest = value - high
    middle = rest.astype(jnp.bfloat16).astype(jnp.float32)
    return high, middle, rest - middle


def pack_kernel(points_ref, weight_ref, potential_ref, out_ref):
    points = points_ref[...]
    wide = points.astype(jnp.float32)
    square = wide * wide
    high = square.astype(jnp.bfloat16)
    low = (square - high.astype(jnp.float32)).astype(jnp.bfloat16)
    ones = jnp.ones((8, points.shape[1]), jnp.bfloat16)
    dims = (((1,), (1,)), ((), ()))
    norms = lax.dot_general(ones, high, dims, preferred_element_type=jnp.float32)
    norms = norms + lax.dot_general(ones, low, dims, preferred_element_type=jnp.float32)
    norms = norms[:1]
    potential = potential_ref[...]
    mass = weight_ref[...] + 0.5 * potential
    offset = (mass - 0.25 * norms) * LOG2E
    own_term = (mass + 0.25 * norms) * LOG2E
    left = three_terms(offset) + three_terms(mass * LOG2E)
    right = three_terms(0.5 * norms - potential) + three_terms(own_term)
    rows = [jnp.concatenate(both, axis=1) for both in zip(left, right)]
    half = jnp.concatenate(rows + [jnp.zeros((2, 2 * LOCAL), jnp.float32)], axis=0)
    out_ref[:LOCAL] = points
    out_ref[LOCAL:] = jnp.concatenate([half, half], axis=0).astype(jnp.bfloat16)


def spread_kernel(pair_ref, out_ref):
    stride = LOCAL + TAIL
    first, second = pair_ref[LOCAL:stride], pair_ref[stride + LOCAL :]
    row = lax.broadcasted_iota(jnp.int32, first.shape, 0)
    tail = jnp.where(row < 8, first.astype(jnp.float32), second.astype(jnp.float32))
    tail = tail.astype(jnp.bfloat16)
    for member in range(MEMBERS):
        out_ref[member, :LOCAL] = pair_ref[:LOCAL]
        out_ref[member, LOCAL : 2 * LOCAL] = pair_ref[stride : stride + LOCAL]
        out_ref[member, 2 * LOCAL :] = tail


def log_sums(row_ref, column_ref, core, offsets):
    line = lax.broadcasted_iota(jnp.int32, (1, 8, LOCAL), 1)

    def gather(tail, first):
        pick = (line >= first) & (line < first + 3)
        return jnp.sum(jnp.where(pick, tail, 0.0), axis=1)

    own = slice(2 * LOCAL, MESSAGE)
    tails = row_ref[:, own].astype(jnp.float32)[:, 8 * core : 8 * core + 8]
    base = gather(tails[:, :, LOCAL:], 0)
    own_term = gather(tails[:, :, LOCAL:], 3)
    least = jnp.min(own_term)
    quarter = jnp.max(own_term - gather(tails[:, :, :LOCAL], 3))
    tails = column_ref[:, own, :LOCAL].astype(jnp.float32)
    mass = jnp.max(jnp.maximum(gather(tails[:, :8], 3), gather(tails[:, 8:], 3)))
    near = mass + quarter - least <= 200.0
    shift = jnp.where(near, least + 90.0, 0.0)

    row = lax.broadcasted_iota(jnp.int32, (TAIL, 2 * LOCAL), 0)
    start = lax.broadcasted_iota(jnp.int32, (TAIL, 2 * LOCAL), 1) // LOCAL * 8
    pick = jnp.where((row >= start) & (row < start + 3), 1.0, 0.0).astype(jnp.bfloat16)
    columns = column_ref.shape[0]
    for block in range(columns):
        both = lax.dot_general(
            column_ref[block, own, :LOCAL],
            pick,
            (((0,), (0,)), ((), ())),
            preferred_element_type=jnp.float32,
        ) - shift
        offsets[block, :LOCAL] = both[:, :LOCAL]
        offsets[block, LOCAL:] = both[:, LOCAL:]

    def scores(block, mine):
        inner = lax.dot_general(
            column_ref[block, : 2 * LOCAL],
            mine,
            (((1,), (1,)), ((), ())),
            preferred_element_type=jnp.float32,
        )
        score = inner * (0.5 * LOG2E) + jnp.concatenate([offsets[block]] * TILE, axis=1)
        return score.reshape(2 * LOCAL // 8, 8, TILE * LOCAL)

    def one_shift(mine):
        total = jnp.zeros((8, TILE * LOCAL), jnp.float32)
        for block in range(columns):
            total = total + jnp.sum(jnp.exp2(scores(block, mine)), axis=0)
        total = jnp.maximum(jnp.sum(total, axis=0, keepdims=True), 2.0**-126)
        return shift + jnp.log2(total)

    def row_maximum(mine):
        def step(block, carry):
            highest, total = carry
            score = scores(block, mine)
            top = jnp.maximum(highest, jnp.max(score, axis=0))
            total = total * jnp.exp2(highest - top) + jnp.sum(jnp.exp2(score - top[None]), axis=0)
            return top, total

        start = jnp.full((8, TILE * LOCAL), -1e30, jnp.float32)
        highest, total = lax.fori_loop(0, columns, step, (start, jnp.zeros_like(start)))
        top = jnp.max(highest, axis=0, keepdims=True)
        total = jnp.sum(total * jnp.exp2(highest - top), axis=0, keepdims=True)
        return top + jnp.log2(total)

    def run(method):
        lines = []
        for step in range(0, row_ref.shape[0], TILE):
            mine = row_ref[step : step + TILE, core * LOCAL : (core + 1) * LOCAL]
            value = method(mine.reshape(TILE * LOCAL, -1))
            lines += [value[:, at * LOCAL : (at + 1) * LOCAL] for at in range(TILE)]
        return jnp.concatenate(lines, axis=0)

    return lax.cond(near, lambda: run(one_shift), lambda: run(row_maximum)), base


def pairs_kernel(final, own_ref, part_ref, *refs):
    if final:
        sum_before, base_before, sum_ref, base_ref, offsets = refs
    else:
        sum_ref, base_ref, offsets = refs
    where = lax.axis_index("narrow") & 1

    def store(value, base):
        base_ref[...] = base
        if not final:
            sum_ref[...] = value
            return
        before = sum_before[...]
        top = jnp.maximum(before, value)
        value = top + jnp.log2(jnp.exp2(before - top) + jnp.exp2(value - top))
        for member in range(MEMBERS):
            sum_ref[member] = value

    @pl.when(where == 0)
    def _():
        store(*log_sums(own_ref, part_ref, 0, offsets))

    @pl.when(where == 1)
    def _():
        value, base = log_sums(part_ref, own_ref, 1, offsets)
        missing = jnp.full((MEMBERS - value.shape[0], LOCAL), -1e30, jnp.float32)
        if final:
            store(
                jnp.concatenate([missing, value], axis=0),
                jnp.concatenate([base_before[:FIRST], base], axis=0),
            )
        else:
            store(
                jnp.concatenate([value, missing], axis=0),
                jnp.concatenate([base, missing], axis=0),
            )


def finish_kernel(parts_ref, base_ref, potential_ref, new_ref, change_ref):
    parts = parts_ref[...]
    top = jnp.max(parts, axis=0)
    value = top + jnp.log2(jnp.sum(jnp.exp2(parts - top[None]), axis=0))
    change = base_ref[...] - (2.0 * LN2) * value
    row = lax.broadcasted_iota(jnp.int32, change.shape, 0)
    mine = jnp.sum(jnp.where(row == lax.axis_index("wide") & (MEMBERS - 1), change, 0.0), axis=0, keepdims=True)
    new_ref[...] = potential_ref[...] + 0.5 * mine
    whole = jnp.sum(jnp.sum(change * change, axis=0, keepdims=True), axis=1, keepdims=True)
    change_ref[...] = jnp.broadcast_to(whole, change_ref.shape)


def norm_kernel(count, parts_ref, out_ref):
    whole = jnp.sum(parts_ref[...], axis=0, keepdims=True)
    out_ref[...] = jnp.sqrt(whole / count + 1e-06)


def call(kernel, outs, *operands, limit=4, **options):
    return pl.pallas_call(
        kernel,
        out_shape=outs,
        compiler_params=pltpu.CompilerParams(vmem_limit_bytes=limit * MIB),
        **options,
    )(*operands)


IN_VMEM = pl.BlockSpec(memory_space=pltpu.VMEM)


def shape(*dims, dtype=jnp.float32):
    return jax.ShapeDtypeStruct(dims, dtype)


def per_device(points, log_point_weight, potential):
    features = points.shape[1]
    narrow = lax.axis_size("narrow")
    own_potential = potential.reshape(1, LOCAL)
    packed = call(
        pack_kernel,
        shape(LOCAL + TAIL, features, dtype=jnp.bfloat16),
        points,
        log_point_weight.reshape(1, LOCAL),
        own_potential,
        limit=60,
    )
    pair = lax.all_gather(
        packed,
        "narrow",
        axis=0,
        tiled=True,
        axis_index_groups=[[at, at + 1] for at in range(0, narrow, 2)],
    )
    message = call(
        spread_kernel, shape(MEMBERS, MESSAGE, features, dtype=jnp.bfloat16), pair, limit=8
    )
    own = lax.all_to_all(
        message,
        AXES,
        0,
        0,
        tiled=True,
        axis_index_groups=row_groups([0]) + column_groups([1]),
    )
    other_core = [(at, at ^ 1) for at in range(narrow)]
    halves = [lax.ppermute(part, "narrow", other_core) for part in jnp.split(own, [FIRST])]
    offsets = [pltpu.VMEM((MEMBERS, 2 * LOCAL, LOCAL), jnp.float32)]
    lines = shape(MEMBERS, LOCAL)
    before = call(
        functools.partial(pairs_kernel, False),
        (lines, lines),
        own,
        halves[0],
        limit=10,
        scratch_shapes=offsets,
    )
    sums, base = call(
        functools.partial(pairs_kernel, True),
        (shape(MEMBERS, MEMBERS, LOCAL), lines),
        own,
        halves[1],
        *before,
        limit=10,
        scratch_shapes=offsets,
    )
    parts = lax.all_to_all(
        sums,
        AXES,
        0,
        0,
        tiled=True,
        axis_index_groups=row_groups([0, 1]),
    )
    new_potential, change = call(
        finish_kernel,
        (shape(1, LOCAL), shape(2 * MEMBERS, LOCAL)),
        parts,
        base,
        own_potential,
        in_specs=[IN_VMEM, IN_VMEM, IN_VMEM],
        out_specs=[IN_VMEM, IN_VMEM],
    )
    changes = lax.all_to_all(
        change, AXES, 0, 0, tiled=True, axis_index_groups=remaining_groups()
    )
    count = LOCAL * lax.axis_size(AXES)
    norm = call(lambda a, b: norm_kernel(count, a, b), shape(1, LOCAL), changes)
    return new_potential.reshape(LOCAL), norm[0, 0]


def solution(mesh):
    in_specs = (P(AXES, None), P(AXES), P(AXES))
    out_specs = (P(AXES), P())
    return jax.shard_map(
        per_device, mesh=mesh, in_specs=in_specs, out_specs=out_specs, check_vma=False
    )
```

```python
import functools
import math

import jax
import jax.numpy as jnp
from jax import lax
from jax.experimental import pallas as pl
from jax.experimental.pallas import tpu as pltpu
from jax.sharding import PartitionSpec as P

LOG2E = math.log2(math.e)
LN2 = math.log(2.0)
AXES = ("wide", "narrow")
SHAPE = (2, 4, 8, 4, 2)
MEMBERS = 16
LOCAL = 128
TAIL = 16
TILE = 4
MESSAGE = 2 * LOCAL + TAIL
MIB = 1024 * 1024
PAIRS = ((0, 1), (2, 3))
CROSS = ((1, 2), (3, 0))


def index(x, y, z, core):
    where = 0
    for size, at in zip(SHAPE, (z % 2, x, y, z // 2, core)):
        where = where * size + at
    return where


def row_groups(cores):
    return [
        [index(x, y, z, core) for x in pair for z in range(8)]
        for pair in PAIRS
        for y in range(8)
        for core in cores
    ]


def column_groups(cores):
    return [
        [index(x, y, z, core) for x in pair for y in range(8)]
        for pair in CROSS
        for z in range(8)
        for core in cores
    ]


def remaining_groups():
    return [
        [index(x, y, z, core) for x in pair for y in range(8) for core in range(2)]
        for pair in CROSS
        for z in range(8)
    ]


def three_terms(value):
    high = value.astype(jnp.bfloat16).astype(jnp.float32)
    rest = value - high
    middle = rest.astype(jnp.bfloat16).astype(jnp.float32)
    return high, middle, rest - middle


def pack_kernel(points_ref, weight_ref, potential_ref, out_ref):
    points = points_ref[...]
    wide = points.astype(jnp.float32)
    square = wide * wide
    high = square.astype(jnp.bfloat16)
    low = (square - high.astype(jnp.float32)).astype(jnp.bfloat16)
    ones = jnp.ones((8, points.shape[1]), jnp.bfloat16)
    dims = (((1,), (1,)), ((), ()))
    norms = lax.dot_general(ones, high, dims, preferred_element_type=jnp.float32)
    norms = norms + lax.dot_general(ones, low, dims, preferred_element_type=jnp.float32)
    norms = norms[:1]
    potential = potential_ref[...]
    mass = weight_ref[...] + 0.5 * potential
    offset = (mass - 0.25 * norms) * LOG2E
    own_term = (mass + 0.25 * norms) * LOG2E
    left = three_terms(offset) + three_terms(mass * LOG2E)
    right = three_terms(0.5 * norms - potential) + three_terms(own_term)
    rows = [jnp.concatenate(both, axis=1) for both in zip(left, right)]
    half = jnp.concatenate(rows + [jnp.zeros((2, 2 * LOCAL), jnp.float32)], axis=0)
    out_ref[:LOCAL] = points
    out_ref[LOCAL:] = jnp.concatenate([half, half], axis=0).astype(jnp.bfloat16)


def spread_kernel(pair_ref, out_ref):
    stride = LOCAL + TAIL
    first, second = pair_ref[LOCAL:stride], pair_ref[stride + LOCAL :]
    row = lax.broadcasted_iota(jnp.int32, first.shape, 0)
    tail = jnp.where(row < 8, first.astype(jnp.float32), second.astype(jnp.float32))
    tail = tail.astype(jnp.bfloat16)
    for member in range(MEMBERS):
        out_ref[member, :LOCAL] = pair_ref[:LOCAL]
        out_ref[member, LOCAL : 2 * LOCAL] = pair_ref[stride : stride + LOCAL]
        out_ref[member, 2 * LOCAL :] = tail


def log_sums(row_ref, column_ref, core, offsets):
    line = lax.broadcasted_iota(jnp.int32, (1, 8, LOCAL), 1)

    def gather(tail, first):
        pick = (line >= first) & (line < first + 3)
        return jnp.sum(jnp.where(pick, tail, 0.0), axis=1)

    own = slice(2 * LOCAL, MESSAGE)
    tails = row_ref[:, own].astype(jnp.float32)[:, 8 * core : 8 * core + 8]
    base = gather(tails[:, :, LOCAL:], 0)
    own_term = gather(tails[:, :, LOCAL:], 3)
    least = jnp.min(own_term)
    quarter = jnp.max(own_term - gather(tails[:, :, :LOCAL], 3))
    tails = column_ref[:, own, :LOCAL].astype(jnp.float32)
    mass = jnp.max(jnp.maximum(gather(tails[:, :8], 3), gather(tails[:, 8:], 3)))
    near = mass + quarter - least <= 200.0
    shift = jnp.where(near, least + 90.0, 0.0)

    row = lax.broadcasted_iota(jnp.int32, (TAIL, 2 * LOCAL), 0)
    start = lax.broadcasted_iota(jnp.int32, (TAIL, 2 * LOCAL), 1) // LOCAL * 8
    pick = jnp.where((row >= start) & (row < start + 3), 1.0, 0.0).astype(jnp.bfloat16)
    columns = column_ref.shape[0]
    for block in range(columns):
        both = lax.dot_general(
            column_ref[block, own, :LOCAL],
            pick,
            (((0,), (0,)), ((), ())),
            preferred_element_type=jnp.float32,
        ) - shift
        offsets[block, :LOCAL] = both[:, :LOCAL]
        offsets[block, LOCAL:] = both[:, LOCAL:]

    def scores(block, mine):
        inner = lax.dot_general(
            column_ref[block, : 2 * LOCAL],
            mine,
            (((1,), (1,)), ((), ())),
            preferred_element_type=jnp.float32,
        )
        score = inner * (0.5 * LOG2E) + jnp.concatenate([offsets[block]] * TILE, axis=1)
        return score.reshape(2 * LOCAL // 8, 8, TILE * LOCAL)

    def one_shift(mine):
        total = jnp.zeros((8, TILE * LOCAL), jnp.float32)
        for block in range(columns):
            total = total + jnp.sum(jnp.exp2(scores(block, mine)), axis=0)
        total = jnp.maximum(jnp.sum(total, axis=0, keepdims=True), 2.0**-126)
        return shift + jnp.log2(total)

    def row_maximum(mine):
        def step(block, carry):
            highest, total = carry
            score = scores(block, mine)
            top = jnp.maximum(highest, jnp.max(score, axis=0))
            total = total * jnp.exp2(highest - top) + jnp.sum(jnp.exp2(score - top[None]), axis=0)
            return top, total

        start = jnp.full((8, TILE * LOCAL), -1e30, jnp.float32)
        highest, total = lax.fori_loop(0, columns, step, (start, jnp.zeros_like(start)))
        top = jnp.max(highest, axis=0, keepdims=True)
        total = jnp.sum(total * jnp.exp2(highest - top), axis=0, keepdims=True)
        return top + jnp.log2(total)

    def run(method):
        lines = []
        for step in range(0, row_ref.shape[0], TILE):
            mine = row_ref[step : step + TILE, core * LOCAL : (core + 1) * LOCAL]
            value = method(mine.reshape(TILE * LOCAL, -1))
            lines += [value[:, at * LOCAL : (at + 1) * LOCAL] for at in range(TILE)]
        return jnp.concatenate(lines, axis=0)

    return lax.cond(near, lambda: run(one_shift), lambda: run(row_maximum)), base


def pairs_kernel(final, own_ref, part_ref, *refs):
    if final:
        sum_before, base_before, sum_ref, base_ref, offsets = refs
    else:
        sum_ref, base_ref, offsets = refs
    where = lax.axis_index("narrow") & 1
    half = MEMBERS // 2

    def store(value, base):
        base_ref[...] = base
        if not final:
            sum_ref[...] = value
            return
        before = sum_before[...]
        top = jnp.maximum(before, value)
        value = top + jnp.log2(jnp.exp2(before - top) + jnp.exp2(value - top))
        for member in range(MEMBERS):
            sum_ref[member] = value

    @pl.when(where == 0)
    def _():
        store(*log_sums(own_ref, part_ref, 0, offsets))

    @pl.when(where == 1)
    def _():
        value, base = log_sums(part_ref, own_ref, 1, offsets)
        missing = jnp.full(value.shape, -1e30, jnp.float32)
        if final:
            store(
                jnp.concatenate([missing, value], axis=0),
                jnp.concatenate([base_before[:half], base], axis=0),
            )
        else:
            store(
                jnp.concatenate([value, missing], axis=0),
                jnp.concatenate([base, base], axis=0),
            )


def finish_kernel(parts_ref, base_ref, potential_ref, new_ref, change_ref):
    parts = parts_ref[...]
    top = jnp.max(parts, axis=0)
    value = top + jnp.log2(jnp.sum(jnp.exp2(parts - top[None]), axis=0))
    change = base_ref[...] - (2.0 * LN2) * value
    wide, narrow = lax.axis_index("wide"), lax.axis_index("narrow")
    z = 2 * (narrow >> 1) + (wide >> 5)
    place = 8 * ((wide >> 3) & 1) + z
    row = lax.broadcasted_iota(jnp.int32, change.shape, 0)
    mine = jnp.sum(jnp.where(row == place, change, 0.0), axis=0, keepdims=True)
    new_ref[...] = potential_ref[...] + 0.5 * mine
    whole = jnp.sum(jnp.sum(change * change, axis=0, keepdims=True), axis=1, keepdims=True)
    change_ref[...] = jnp.broadcast_to(whole, change_ref.shape)


def norm_kernel(count, parts_ref, out_ref):
    whole = jnp.sum(parts_ref[...], axis=0, keepdims=True)
    out_ref[...] = jnp.sqrt(whole / count + 1e-06)


def call(kernel, outs, *operands, limit=4, **options):
    return pl.pallas_call(
        kernel,
        out_shape=outs,
        compiler_params=pltpu.CompilerParams(vmem_limit_bytes=limit * MIB),
        **options,
    )(*operands)


IN_VMEM = pl.BlockSpec(memory_space=pltpu.VMEM)


def shape(*dims, dtype=jnp.float32):
    return jax.ShapeDtypeStruct(dims, dtype)


def per_device(points, log_point_weight, potential):
    features = points.shape[1]
    narrow = lax.axis_size("narrow")
    own_potential = potential.reshape(1, LOCAL)
    packed = call(
        pack_kernel,
        shape(LOCAL + TAIL, features, dtype=jnp.bfloat16),
        points,
        log_point_weight.reshape(1, LOCAL),
        own_potential,
        limit=60,
    )
    pair = lax.all_gather(
        packed,
        "narrow",
        axis=0,
        tiled=True,
        axis_index_groups=[[at, at + 1] for at in range(0, narrow, 2)],
    )
    message = call(
        spread_kernel, shape(MEMBERS, MESSAGE, features, dtype=jnp.bfloat16), pair, limit=8
    )
    own = lax.all_to_all(
        message,
        AXES,
        0,
        0,
        tiled=True,
        axis_index_groups=row_groups([0]) + column_groups([1]),
    )
    other_core = [(at, at ^ 1) for at in range(narrow)]
    halves = [lax.ppermute(part, "narrow", other_core) for part in jnp.split(own, 2)]
    offsets = [pltpu.VMEM((MEMBERS, 2 * LOCAL, LOCAL), jnp.float32)]
    lines = shape(MEMBERS, LOCAL)
    before = call(
        functools.partial(pairs_kernel, False),
        (lines, lines),
        own,
        halves[0],
        limit=10,
        scratch_shapes=offsets,
    )
    sums, base = call(
        functools.partial(pairs_kernel, True),
        (shape(MEMBERS, MEMBERS, LOCAL), lines),
        own,
        halves[1],
        *before,
        limit=10,
        scratch_shapes=offsets,
    )
    parts = lax.all_to_all(
        sums,
        AXES,
        0,
        0,
        tiled=True,
        axis_index_groups=row_groups([0, 1]),
    )
    new_potential, change = call(
        finish_kernel,
        (shape(1, LOCAL), shape(2 * MEMBERS, LOCAL)),
        parts,
        base,
        own_potential,
        in_specs=[IN_VMEM, IN_VMEM, IN_VMEM],
        out_specs=[IN_VMEM, IN_VMEM],
    )
    changes = lax.all_to_all(
        change, AXES, 0, 0, tiled=True, axis_index_groups=remaining_groups()
    )
    count = LOCAL * lax.axis_size(AXES)
    norm = call(lambda a, b: norm_kernel(count, a, b), shape(1, LOCAL), changes)
    return new_potential.reshape(LOCAL), norm[0, 0]


def solution(mesh):
    in_specs = (P(AXES, None), P(AXES), P(AXES))
    out_specs = (P(AXES), P())
    return jax.shard_map(
        per_device, mesh=mesh, in_specs=in_specs, out_specs=out_specs, check_vma=False
    )
```
